32 devices in a mesh: expert: 16 (over z, y, x), tensor: 2 (over core).
Axes of the slice: x: 2, y: 2, z: 4, core: 2. Of those that a mesh axis runs over, the one named last changes fastest.
Arguments:
- tokens: bfloat16 [8192, 1024], P('expert', 'tensor'), may hold values from -6 to 6
- expert_ids: int32 [8192], P('expert'), may hold values from 0 to 15, as said below
- gate_scale: float32 [8192], P('expert'), may hold values from 0.25 to 1
- gate_weight: bfloat16 [16, 1024, 6144], P('expert', None, 'tensor'), may hold values from -0.1875 to 0.1875
- up_weight: bfloat16 [16, 1024, 6144], P('expert', None, 'tensor'), may hold values from -0.1875 to 0.1875
- down_weight: bfloat16 [16, 6144, 1024], P('expert', 'tensor'), may hold values from -0.109375 to 0.109375
Outputs:
- combined: bfloat16 [8192, 1024], P('expert', 'tensor')
The draws below stay inside these ranges and needn't reach their ends.
Inputs may be any that keep to these rules, and one draw needn't show every extreme that they name: `expert_ids`: among the 512 tokens of one index of expert, no expert id appears more than 64 times, and one expert, the same for every index, appears exactly 64 times in each.
All inputs are finite; a program needn't handle non-finite values.
Results may differ from the reference program's by a relative error of at most 0.02.
Values may be sent and summed in bfloat16 or wider, within the bound.
No kernel may reach another device: no remote copies, remote signals or barrier semaphores. Data moves between devices by JAX's collectives and lax.ppermute only.
A program may use at most 64 MiB of HBM per device.

```python
import jax
import jax.numpy as jnp
from jax import lax

D = 1024
FF = 6144
TOK_DEV = 512
EXPERTS = 16
TOKENS = 8192
CAP = 64
SLOTS = 1024
HID_DEV = 3072
N_TENSOR = 2


def draw_expert_ids(key, part):
    hot_key, rest_key = jax.random.split(key)
    hot = jax.random.randint(hot_key, (), 0, EXPERTS).astype(jnp.int32)

    def one_block(block_key):
        first_key, second_key = jax.random.split(block_key)
        chosen = jax.random.permutation(first_key, (EXPERTS - 1) * CAP)[:TOK_DEV - CAP]
        others = (chosen // CAP).astype(jnp.int32)
        others = others + (others >= hot).astype(jnp.int32)
        block_ids = jnp.concatenate([jnp.full((CAP,), hot, jnp.int32), others])
        return jax.random.permutation(second_key, block_ids)
    block_keys = jax.random.split(rest_key, TOKENS // TOK_DEV)
    return jax.vmap(one_block)(block_keys).reshape(TOKENS).astype(jnp.int32)


def with_spikes(drawn, stream_key, source, target, blocks, factor):
    owner, partner = [(jnp.arange(drawn.shape[dim]) // (drawn.shape[dim] // blocks)).reshape([-1 if axis == dim else 1 for axis in range(drawn.ndim)]) for dim in (source, target)]
    chosen = jax.random.permutation(stream_key, blocks)[partner]
    strong = (owner == chosen) | (owner == (partner + blocks // 2) % blocks)
    return jnp.where(strong, factor * drawn, drawn)


def levels(key, extent, shards, low, high):
    gain, own = 1.0, jax.random.fold_in(key, 6)
    for dim, parts in shards:
        steps = jnp.exp(jax.random.uniform(jax.random.fold_in(own, dim), (parts,), jnp.float32, low / len(shards), high / len(shards)))
        gain = gain * jnp.repeat(steps, extent[dim] // parts).reshape([-1 if axis == dim else 1 for axis in range(len(extent))])
    return gain


def bell_draw(stream_key, shape, width, reach, pieces=(), kind=jnp.bfloat16):
    values = width * jax.random.normal(stream_key, shape, jnp.float32)
    if pieces:
        values = values * levels(stream_key, shape, pieces, -0.22, 0.18)
    return jnp.clip(values, -reach, reach).astype(kind)


def heavy_noise(own_key, extent, deviation, most, cuts, heavy, kind=jnp.bfloat16):
    array = deviation * jax.random.normal(own_key, extent, jnp.float32)
    if cuts:
        array = array * levels(own_key, extent, cuts, -0.22, 0.18)
    return jnp.clip(with_spikes(array, jax.random.fold_in(own_key, 3), *heavy), -most, most).astype(kind)


def setup_inputs(seed: int = 0) -> dict:
    splits = jax.random.split(jax.random.key(seed), 7)
    return {
        "tokens": bell_draw(splits[0], (TOKENS, D), 1.0, 6.0, ((0, 16), (1, 2))),
        "expert_ids": draw_expert_ids(jax.random.fold_in(splits[6], 71), 0),
        "gate_scale": jnp.clip(0.25 + 0.75 * jax.random.uniform(splits[2], (TOKENS,), jnp.float32) ** levels(splits[2], (TOKENS,), ((0, 16),), -0.2, 0.2), 0.25, 1.0),
        "gate_weight": bell_draw(splits[3], (EXPERTS, D, FF), D ** -0.5, 0.1875, ((0, 16), (2, 2))),
        "up_weight": bell_draw(splits[4], (EXPERTS, D, FF), D ** -0.5, 0.1875, ((0, 16), (2, 2))),
        "down_weight": heavy_noise(splits[5], (EXPERTS, FF, D), FF ** -0.5, 0.109375, ((0, 16), (1, 2)), (1, 2, 2, 2.0)),
    }


def expert_rows(rows, w_gate, w_up, w_down):
    gate = jnp.dot(rows, w_gate, preferred_element_type=jnp.float32)
    up = jnp.dot(rows, w_up, preferred_element_type=jnp.float32)
    hidden = (jax.nn.silu(gate) * up).astype(jnp.bfloat16)
    hid_slices = hidden.astype(jnp.float32).reshape(rows.shape[0], N_TENSOR, HID_DEV)
    down_slices = w_down.astype(jnp.float32).reshape(N_TENSOR, HID_DEV, D)
    partials = jnp.einsum("rtf,tfd->trd", hid_slices, down_slices).astype(jnp.bfloat16)
    return jnp.sum(partials.astype(jnp.float32), axis=0).astype(jnp.bfloat16)


def reference(tokens, expert_ids, gate_scale, gate_weight, up_weight, down_weight):
    order = jnp.argsort(expert_ids, stable=True).astype(jnp.int32)
    sorted_ids = expert_ids[order]
    owners = jnp.arange(EXPERTS, dtype=jnp.int32)
    counts = jnp.sum((expert_ids[:, None] == owners[None, :]).astype(jnp.int32), axis=0)
    starts = (jnp.cumsum(counts) - counts).astype(jnp.int32)
    padded = jnp.concatenate([tokens[order], jnp.zeros((SLOTS, D), tokens.dtype)], axis=0)

    def one_expert(index):
        rows = lax.dynamic_slice_in_dim(padded, starts[index], SLOTS, 0)
        return expert_rows(rows, gate_weight[index], up_weight[index], down_weight[index])

    results = lax.map(one_expert, owners)
    position = jnp.arange(TOKENS, dtype=jnp.int32) - starts[sorted_ids]
    flat = results.reshape(EXPERTS * SLOTS, D)
    sorted_out = flat[(sorted_ids * SLOTS + position).astype(jnp.int32)]
    unsorted = jnp.zeros_like(sorted_out).at[order].set(sorted_out)
    return (gate_scale[:, None] * unsorted.astype(jnp.float32)).astype(jnp.bfloat16)
```

```python
import functools

import jax
import jax.numpy as jnp
from jax import lax
from jax.experimental import pallas as pl
from jax.experimental.pallas import tpu as pltpu
from jax.sharding import PartitionSpec as P

F32 = jnp.float32
BF16 = jnp.bfloat16
MIB = 1 << 20


def vmem():
    return pl.BlockSpec(memory_space=pltpu.VMEM)


def params(limit_mib):
    return pltpu.CompilerParams(vmem_limit_bytes=limit_mib * MIB)


def chunk_sizes(capacity):
    if capacity >= 32:
        return (capacity // 2, capacity // 2)
    return (capacity,)


def dispatch_kernel(n_expert, chunks, ids_ref, tok_ref, *out_refs):
    n_tok = tok_ref.shape[0]
    ids = ids_ref[...]
    owner = lax.broadcasted_iota(jnp.int32, (n_expert, n_tok), 0)
    onehot = (owner == ids).astype(F32)
    before = lax.broadcasted_iota(jnp.int32, (n_tok, n_tok), 0) < lax.broadcasted_iota(jnp.int32, (n_tok, n_tok), 1)
    earlier = jnp.dot(onehot.astype(BF16), before.astype(F32).astype(BF16), preferred_element_type=F32)
    rank = jnp.sum(earlier * onehot, axis=0, keepdims=True).astype(jnp.int32)
    low = 0
    for size, out_ref in zip(chunks, out_refs):
        inside = (rank >= low) & (rank < low + size)
        target = jnp.where(inside, ids * size + (rank - low), -1)
        slot = lax.broadcasted_iota(jnp.int32, (n_expert * size, n_tok), 0)
        pick = (slot == target).astype(F32).astype(BF16)
        out_ref[...] = jnp.dot(pick, tok_ref[...], preferred_element_type=F32).astype(BF16)
        low += size


def dispatch(ids, tokens, n_expert, chunks):
    n_tok, width = tokens.shape
    return pl.pallas_call(
        functools.partial(dispatch_kernel, n_expert, chunks),
        out_shape=[jax.ShapeDtypeStruct((n_expert * size, width), BF16) for size in chunks],
        in_specs=[vmem(), vmem()],
        out_specs=[vmem() for _ in chunks],
        compiler_params=params(24),
        name="dispatch",
    )(ids.reshape(1, n_tok), tokens)


def combine_map_kernel(n_expert, chunks, ids_ref, *out_refs):
    n_tok = ids_ref.shape[0]
    ids = ids_ref[...]
    owner = lax.broadcasted_iota(jnp.int32, (n_tok, n_expert), 1)
    onehot = (owner == ids).astype(F32)
    before = lax.broadcasted_iota(jnp.int32, (n_tok, n_tok), 1) < lax.broadcasted_iota(jnp.int32, (n_tok, n_tok), 0)
    earlier = jnp.dot(before.astype(F32).astype(BF16), onehot.astype(BF16), preferred_element_type=F32)
    rank = jnp.sum(earlier * onehot, axis=1, keepdims=True).astype(jnp.int32)
    low = 0
    for size, out_ref in zip(chunks, out_refs):
        inside = (rank >= low) & (rank < low + size)
        target = jnp.where(inside, ids * size + (rank - low), -1)
        slot = lax.broadcasted_iota(jnp.int32, (n_tok, n_expert * size), 1)
        out_ref[...] = (slot == target).astype(F32).astype(BF16)
        low += size


def combine_map(ids, n_expert, chunks):
    n_tok = ids.shape[0]
    return pl.pallas_call(
        functools.partial(combine_map_kernel, n_expert, chunks),
        out_shape=[jax.ShapeDtypeStruct((n_tok, n_expert * size), BF16) for size in chunks],
        in_specs=[vmem()],
        out_specs=[vmem() for _ in chunks],
        compiler_params=params(24),
        name="combine_map",
    )(ids.reshape(n_tok, 1))


def pick_kernel(map_ref, back_ref, out_ref):
    out_ref[...] = jnp.dot(map_ref[...], back_ref[...], preferred_element_type=F32).astype(BF16)


def pick(pick_map, back):
    return pl.pallas_call(
        pick_kernel,
        out_shape=jax.ShapeDtypeStruct((pick_map.shape[0], back.shape[1]), BF16),
        in_specs=[vmem(), vmem()],
        out_specs=vmem(),
        compiler_params=params(16),
        name="pick",
    )(pick_map, back)


def finish_kernel(n_part, map_ref, back_ref, scale_ref, *refs):
    total = jnp.dot(map_ref[...], back_ref[...], preferred_element_type=F32)
    for part_ref in refs[:n_part]:
        total = total + part_ref[...].astype(F32)
    refs[n_part][...] = (scale_ref[...] * total).astype(BF16)


def finish(pick_map, back, scale, parts):
    n_tok = pick_map.shape[0]
    return pl.pallas_call(
        functools.partial(finish_kernel, len(parts)),
        out_shape=jax.ShapeDtypeStruct((n_tok, back.shape[1]), BF16),
        in_specs=[vmem() for _ in range(3 + len(parts))],
        out_specs=vmem(),
        compiler_params=params(16),
        name="finish",
    )(pick_map, back, scale.reshape(n_tok, 1), *parts)


def expert_kernel(n_tensor, n_block, where_ref, *refs):
    part_refs = refs[:n_tensor]
    sources = refs[n_tensor:n_tensor + 3]
    out_refs = refs[n_tensor + 3:2 * n_tensor + 3]
    total_refs = refs[2 * n_tensor + 3:3 * n_tensor + 3]
    gate_ref, up_ref, down_ref, arrived = refs[3 * n_tensor + 3:]
    ring, _, block = gate_ref.shape
    width = part_refs[0].shape[1]
    me = where_ref[0]

    def columns(shift):
        return pl.ds(pl.multiple_of(lax.rem(me + shift, n_tensor) * width, width), width)

    def fetches(step):
        slot = lax.rem(step, ring)
        cut = pl.ds(pl.multiple_of(step * block, block), block)
        return [
            pltpu.make_async_copy(sources[0].at[0, :, cut], gate_ref.at[slot], arrived.at[slot, 0]),
            pltpu.make_async_copy(sources[1].at[0, :, cut], up_ref.at[slot], arrived.at[slot, 1]),
            pltpu.make_async_copy(sources[2].at[0, cut, :], down_ref.at[slot], arrived.at[slot, 2]),
        ]

    def start(step):
        for fetch in fetches(step):
            fetch.start()

    def product(weight_ref, slot):
        total = None
        for shift, part_ref in enumerate(part_refs):
            term = jnp.dot(part_ref[...], weight_ref[slot, columns(shift), :], preferred_element_type=F32)
            total = term if total is None else total + term
        return total

    def work(step, first):
        gate_here, up_here, down_here = fetches(step)
        slot = lax.rem(step, ring)
        gate_here.wait()
        gate = product(gate_ref, slot)
        up_here.wait()
        up = product(up_ref, slot)
        hidden = (gate / (1.0 + jnp.exp(-gate)) * up).astype(BF16)
        down_here.wait()
        for shift, total_ref in enumerate(total_refs):
            share = jnp.dot(hidden, down_ref[slot, :, columns(shift)], preferred_element_type=F32)
            if first:
                total_ref[...] = share
            else:
                total_ref[...] += share

    for step in range(min(ring, n_block)):
        start(step)
    if UNROLL:
        for step in range(n_block):
            work(step, step == 0)
            if step + ring < n_block:
                start(step + ring)
    else:
        for total_ref in total_refs:
            total_ref[...] = jnp.zeros_like(total_ref)

        @pl.loop(0, n_block)
        def _(step):
            work(step, False)

            @pl.when(step + ring < n_block)
            def _():
                start(step + ring)
    for total_ref, out_ref in zip(total_refs, out_refs):
        out_ref[...] = total_ref[...].astype(BF16)


BLOCK = 1024
RING = 2
UNROLL = False
LIMIT = 24


def expert_rows(where, parts, weights):
    n_tensor = len(parts)
    rows, width = parts[0].shape
    depth, hidden = weights[0].shape[1:]
    block = BLOCK if hidden % BLOCK == 0 else 256
    n_block = hidden // block
    ring = min(RING, n_block)
    hbm = pl.BlockSpec(memory_space=pltpu.HBM)
    return pl.pallas_call(
        functools.partial(expert_kernel, n_tensor, n_block),
        out_shape=[jax.ShapeDtypeStruct((rows, width), BF16) for _ in parts],
        in_specs=[pl.BlockSpec(memory_space=pltpu.SMEM)] + [vmem() for _ in parts] + [hbm, hbm, hbm],
        out_specs=[vmem() for _ in parts],
        scratch_shapes=[pltpu.VMEM((rows, width), F32) for _ in parts]
        + [
            pltpu.VMEM((ring, depth, block), BF16),
            pltpu.VMEM((ring, depth, block), BF16),
            pltpu.VMEM((ring, block, depth), BF16),
            pltpu.SemaphoreType.DMA((ring, 3)),
        ],
        compiler_params=params(LIMIT),
        cost_estimate=pl.CostEstimate(
            flops=6 * rows * depth * hidden, bytes_accessed=6 * depth * hidden, transcendentals=rows * hidden
        ),
        name="expert_rows",
    )(where, *parts, *[pltpu.with_memory_space_constraint(weight, pltpu.HBM) for weight in weights])


def add_kernel(*refs):
    total = refs[0][...].astype(F32)
    for ref in refs[1:-1]:
        total = total + ref[...].astype(F32)
    refs[-1][...] = total.astype(BF16)


def add(shares):
    return pl.pallas_call(
        add_kernel,
        out_shape=jax.ShapeDtypeStruct(shares[0].shape, BF16),
        in_specs=[vmem() for _ in shares],
        out_specs=vmem(),
        compiler_params=params(8),
        name="add_shares",
    )(*shares)


def order_swap(n_expert):
    return n_expert // 4 if n_expert & (n_expert - 1) == 0 else 0


def exchange(rows, n_expert):
    size = rows.shape[0] // n_expert
    swap = order_swap(n_expert)
    moved = lax.all_to_all(
        rows.reshape(n_expert, size, -1),
        "expert",
        split_axis=0,
        concat_axis=0,
        axis_index_groups=[[j ^ swap for j in range(n_expert)]],
        tiled=True,
    )
    return moved.reshape(rows.shape)


def shards(tokens, expert_ids, gate_scale, gate_weight, up_weight, down_weight):
    n_expert = lax.axis_size("expert")
    n_tensor = lax.axis_size("tensor")
    chunks = chunk_sizes(2 * tokens.shape[0] // n_expert)
    where = lax.axis_index("tensor").astype(jnp.int32).reshape(1)

    def shifted(rows, shift):
        return lax.ppermute(rows, "tensor", [(i, (i - shift) % n_tensor) for i in range(n_tensor)])

    expert_ids = expert_ids ^ order_swap(n_expert)
    outgoing = dispatch(expert_ids, tokens, n_expert, chunks)
    maps = combine_map(expert_ids, n_expert, chunks)
    weights = (gate_weight, up_weight, down_weight)
    backs = []
    for rows in outgoing:
        arrived = exchange(rows, n_expert)
        parts = [arrived] + [shifted(arrived, shift) for shift in range(1, n_tensor)]
        shares = expert_rows(where, parts, weights)
        total = add([shares[0]] + [shifted(shares[shift], -shift) for shift in range(1, n_tensor)])
        backs.append(exchange(total, n_expert))
    picked = [pick(pick_map, back) for pick_map, back in zip(maps[:-1], backs[:-1])]
    return finish(maps[-1], backs[-1], gate_scale, picked)


def solution(mesh):
    in_specs = (
        P("expert", "tensor"),
        P("expert"),
        P("expert"),
        P("expert", None, "tensor"),
        P("expert", None, "tensor"),
        P("expert", "tensor", None),
    )
    out_specs = P("expert", "tensor")
    return jax.shard_map(shards, mesh=mesh, in_specs=in_specs, out_specs=out_specs, check_vma=False)
```

```python
import functools

import jax
import jax.numpy as jnp
from jax import lax
from jax.experimental import pallas as pl
from jax.experimental.pallas import tpu as pltpu
from jax.sharding import PartitionSpec as P

F32 = jnp.float32
BF16 = jnp.bfloat16
MIB = 1 << 20


def vmem():
    return pl.BlockSpec(memory_space=pltpu.VMEM)


def in_hbm(array):
    return pltpu.with_memory_space_constraint(array, pltpu.HBM)


def exchange_order(n_expert):
    if n_expert == 16:
        return [10, 4, 9, 8, 5, 6, 11, 7, 12, 0, 13, 1, 14, 2, 15, 3]
    if n_expert % 4:
        return list(range(n_expert))
    quarter = [list(range(q * n_expert // 4, (q + 1) * n_expert // 4)) for q in range(4)]
    return [e for first, second in ((1, 2), (0, 3)) for pair in zip(quarter[first], quarter[second]) for e in pair]


def exchange_place(expert, n_expert):
    place = jnp.zeros_like(expert)
    for index, owner in enumerate(exchange_order(n_expert)):
        place = jnp.where(expert == owner, index, place)
    return place


def params(limit_mib):
    return pltpu.CompilerParams(vmem_limit_bytes=limit_mib * MIB)


def chunk_sizes(capacity):
    if capacity >= 32:
        return (capacity // 2, capacity // 2)
    return (capacity,)


def dispatch_kernel(n_expert, chunks, ids_hbm, tok_hbm, *refs):
    out_refs = refs[:len(chunks)]
    ids_ref, tok_ref, *stage_refs, arrived = refs[len(chunks):]
    copies = [
        pltpu.make_async_copy(ids_hbm, ids_ref, arrived.at[0]),
        pltpu.make_async_copy(tok_hbm, tok_ref, arrived.at[1]),
    ]
    for copy in copies:
        copy.start()
    n_tok = tok_ref.shape[0]
    owner = lax.broadcasted_iota(jnp.int32, (n_expert, n_tok), 0)
    before = lax.broadcasted_iota(jnp.int32, (n_tok, n_tok), 0) < lax.broadcasted_iota(jnp.int32, (n_tok, n_tok), 1)
    before = before.astype(F32).astype(BF16)
    copies[0].wait()
    ids = exchange_place(ids_ref[...], n_expert)
    onehot = (owner == ids).astype(F32)
    earlier = jnp.dot(onehot.astype(BF16), before, preferred_element_type=F32)
    rank = jnp.sum(earlier * onehot, axis=0, keepdims=True).astype(jnp.int32)
    picks = []
    low = 0
    for size in chunks:
        inside = (rank >= low) & (rank < low + size)
        target = jnp.where(inside, ids * size + (rank - low), -1)
        slot = lax.broadcasted_iota(jnp.int32, (n_expert * size, n_tok), 0)
        picks.append((slot == target).astype(F32).astype(BF16))
        low += size
    copies[1].wait()
    leaving = []
    for index in reversed(range(len(chunks))):
        rows = jnp.dot(picks[index], tok_ref[...], preferred_element_type=F32).astype(BF16)
        if index == 0:
            out_refs[0][...] = rows
        else:
            stage_refs[index - 1][...] = rows
            leaving.append(pltpu.make_async_copy(stage_refs[index - 1], out_refs[index], arrived.at[1 + index]))
            leaving[-1].start()
    for copy in leaving:
        copy.wait()


def dispatch(ids, tokens, n_expert, chunks):
    n_tok, width = tokens.shape
    hbm = pl.BlockSpec(memory_space=pltpu.HBM)
    return pl.pallas_call(
        functools.partial(dispatch_kernel, n_expert, chunks),
        out_shape=[jax.ShapeDtypeStruct((n_expert * size, width), BF16) for size in chunks],
        in_specs=[hbm, hbm],
        out_specs=[vmem()] + [hbm for _ in chunks[1:]],
        scratch_shapes=[pltpu.VMEM((1, n_tok), jnp.int32), pltpu.VMEM((n_tok, width), BF16)]
        + [pltpu.VMEM((n_expert * size, width), BF16) for size in chunks[1:]]
        + [pltpu.SemaphoreType.DMA((1 + len(chunks),))],
        compiler_params=params(24),
        name="dispatch",
    )(in_hbm(ids.reshape(1, n_tok)), in_hbm(tokens))


def combine_map_kernel(n_expert, chunks, ids_ref, *out_refs):
    n_tok = ids_ref.shape[0]
    ids = exchange_place(ids_ref[...], n_expert)
    owner = lax.broadcasted_iota(jnp.int32, (n_tok, n_expert), 1)
    onehot = (owner == ids).astype(F32)
    before = lax.broadcasted_iota(jnp.int32, (n_tok, n_tok), 1) < lax.broadcasted_iota(jnp.int32, (n_tok, n_tok), 0)
    earlier = jnp.dot(before.astype(F32).astype(BF16), onehot.astype(BF16), preferred_element_type=F32)
    rank = jnp.sum(earlier * onehot, axis=1, keepdims=True).astype(jnp.int32)
    low = 0
    for size, out_ref in zip(chunks, out_refs):
        inside = (rank >= low) & (rank < low + size)
        target = jnp.where(inside, ids * size + (rank - low), -1)
        slot = lax.broadcasted_iota(jnp.int32, (n_tok, n_expert * size), 1)
        out_ref[...] = (slot == target).astype(F32).astype(BF16)
        low += size


def combine_map(ids, n_expert, chunks):
    n_tok = ids.shape[0]
    return pl.pallas_call(
        functools.partial(combine_map_kernel, n_expert, chunks),
        out_shape=[jax.ShapeDtypeStruct((n_tok, n_expert * size), BF16) for size in chunks],
        in_specs=[vmem()],
        out_specs=[vmem() for _ in chunks],
        compiler_params=params(24),
        name="combine_map",
    )(ids.reshape(n_tok, 1))


def pick_kernel(map_ref, back_ref, out_ref):
    out_ref[...] = jnp.dot(map_ref[...], back_ref[...], preferred_element_type=F32).astype(BF16)


def pick(pick_map, back):
    return pl.pallas_call(
        pick_kernel,
        out_shape=jax.ShapeDtypeStruct((pick_map.shape[0], back.shape[1]), BF16),
        in_specs=[vmem(), vmem()],
        out_specs=vmem(),
        compiler_params=params(16),
        name="pick",
    )(pick_map, back)


def finish_kernel(n_part, map_ref, back_ref, scale_ref, *refs):
    part_refs = refs[:n_part]
    out_hbm, stage_ref, left = refs[n_part:]
    copies = []
    for index, cut in enumerate(row_cuts(stage_ref.shape[0])):
        total = jnp.dot(map_ref[cut, :], back_ref[...], preferred_element_type=F32)
        for part_ref in part_refs:
            total = total + part_ref[cut, :].astype(F32)
        stage_ref[cut, :] = (scale_ref[cut, :] * total).astype(BF16)
        copies.append(pltpu.make_async_copy(stage_ref.at[cut, :], out_hbm.at[cut, :], left.at[index]))
        copies[-1].start()
    for copy in copies:
        copy.wait()


def finish(pick_map, back, scale, parts):
    n_tok = pick_map.shape[0]
    shape = (n_tok, back.shape[1])
    return pl.pallas_call(
        functools.partial(finish_kernel, len(parts)),
        out_shape=jax.ShapeDtypeStruct(shape, BF16),
        in_specs=[vmem() for _ in range(3 + len(parts))],
        out_specs=pl.BlockSpec(memory_space=pltpu.HBM),
        scratch_shapes=[pltpu.VMEM(shape, BF16), pltpu.SemaphoreType.DMA((len(row_cuts(n_tok)),))],
        compiler_params=params(16),
        name="finish",
    )(pick_map, back, scale.reshape(n_tok, 1), *parts)


def expert_kernel(n_tensor, blocks, where_ref, *refs):
    part_refs = refs[:n_tensor]
    sources = refs[n_tensor:n_tensor + 3]
    out_refs = refs[n_tensor + 3:2 * n_tensor + 3]
    gate_ref, up_ref, down_ref, rows_ref, hidden_ref, arrived = refs[2 * n_tensor + 3:]
    width = part_refs[0].shape[1]
    me = where_ref[0]

    def columns(shift):
        return pl.ds(pl.multiple_of(lax.rem(me + shift, n_tensor) * width, width), width)

    fetches = []
    low = 0
    for step, size in enumerate(blocks):
        cut = pl.ds(low, size)
        fetches.append(
            (
                cut,
                pltpu.make_async_copy(sources[0].at[0, :, cut], gate_ref.at[:, cut], arrived.at[2 * step]),
                pltpu.make_async_copy(sources[1].at[0, :, cut], up_ref.at[:, cut], arrived.at[2 * step + 1]),
            )
        )
        low += size
    down_here = pltpu.make_async_copy(sources[2].at[0], down_ref, arrived.at[2 * len(blocks)])
    for _, gate_here, up_here in fetches:
        gate_here.start()
        up_here.start()
    down_here.start()
    for shift, part_ref in enumerate(part_refs):
        rows_ref[:, columns(shift)] = part_ref[...]
    for cut, gate_here, up_here in fetches:
        rows = rows_ref[...]
        gate_here.wait()
        gate = jnp.dot(rows, gate_ref[:, cut], preferred_element_type=F32)
        up_here.wait()
        up = jnp.dot(rows, up_ref[:, cut], preferred_element_type=F32)
        hidden_ref[:, cut] = (gate / (1.0 + jnp.exp(-gate)) * up).astype(BF16)
    down_here.wait()
    for shift, out_ref in enumerate(out_refs):
        share = jnp.dot(hidden_ref[...], down_ref[:, columns(shift)], preferred_element_type=F32)
        out_ref[...] = share.astype(BF16)


def expert_rows(where, parts, weights):
    n_tensor = len(parts)
    rows, width = parts[0].shape
    depth, hidden = weights[0].shape[1:]
    first = hidden // 3 // 128 * 128
    blocks = (first, hidden - first)
    hbm = pl.BlockSpec(memory_space=pltpu.HBM)
    return pl.pallas_call(
        functools.partial(expert_kernel, n_tensor, blocks),
        out_shape=[jax.ShapeDtypeStruct((rows, width), BF16) for _ in parts],
        in_specs=[pl.BlockSpec(memory_space=pltpu.SMEM)] + [vmem() for _ in parts] + [hbm, hbm, hbm],
        out_specs=[vmem() for _ in parts],
        scratch_shapes=[
            pltpu.VMEM((depth, hidden), BF16),
            pltpu.VMEM((depth, hidden), BF16),
            pltpu.VMEM((hidden, depth), BF16),
            pltpu.VMEM((rows, depth), BF16),
            pltpu.VMEM((rows, hidden), BF16),
            pltpu.SemaphoreType.DMA((2 * len(blocks) + 1,)),
        ],
        compiler_params=params(44),
        cost_estimate=pl.CostEstimate(
            flops=6 * rows * depth * hidden, bytes_accessed=6 * depth * hidden, transcendentals=rows * hidden
        ),
        name="expert_rows",
    )(where, *parts, *[in_hbm(weight) for weight in weights])


def row_cuts(rows):
    cut = rows // 4 if rows % 64 == 0 else rows
    return [pl.ds(low, cut) for low in range(0, rows, cut)]


def add_kernel(*refs):
    *share_refs, out_hbm, stage_ref, left = refs
    copies = []
    for index, cut in enumerate(row_cuts(stage_ref.shape[0])):
        total = share_refs[0][cut, :].astype(F32)
        for share_ref in share_refs[1:]:
            total = total + share_ref[cut, :].astype(F32)
        stage_ref[cut, :] = total.astype(BF16)
        copies.append(pltpu.make_async_copy(stage_ref.at[cut, :], out_hbm.at[cut, :], left.at[index]))
        copies[-1].start()
    for copy in copies:
        copy.wait()


def add(shares):
    shape = shares[0].shape
    return pl.pallas_call(
        add_kernel,
        out_shape=jax.ShapeDtypeStruct(shape, BF16),
        in_specs=[vmem() for _ in shares],
        out_specs=pl.BlockSpec(memory_space=pltpu.HBM),
        scratch_shapes=[pltpu.VMEM(shape, BF16), pltpu.SemaphoreType.DMA((len(row_cuts(shape[0])),))],
        compiler_params=params(8),
        name="add_shares",
    )(*shares)


def exchange(rows, n_expert):
    size = rows.shape[0] // n_expert
    moved = lax.all_to_all(
        rows.reshape(n_expert, size, -1),
        "expert",
        split_axis=0,
        concat_axis=0,
        axis_index_groups=[exchange_order(n_expert)],
        tiled=True,
    )
    return moved.reshape(rows.shape)


def shards(tokens, expert_ids, gate_scale, gate_weight, up_weight, down_weight):
    n_expert = lax.axis_size("expert")
    n_tensor = lax.axis_size("tensor")
    chunks = chunk_sizes(2 * tokens.shape[0] // n_expert)
    where = lax.axis_index("tensor").astype(jnp.int32).reshape(1)

    def shifted(rows, shift):
        return lax.ppermute(rows, "tensor", [(i, (i - shift) % n_tensor) for i in range(n_tensor)])

    outgoing = dispatch(expert_ids, tokens, n_expert, chunks)
    maps = combine_map(expert_ids, n_expert, chunks)
    weights = (gate_weight, up_weight, down_weight)
    backs = []
    for rows in outgoing:
        arrived = exchange(rows, n_expert)
        parts = [arrived] + [shifted(arrived, shift) for shift in range(1, n_tensor)]
        shares = expert_rows(where, parts, weights)
        total = add([shares[0]] + [shifted(shares[shift], -shift) for shift in range(1, n_tensor)])
        backs.append(exchange(total, n_expert))
    picked = [pick(pick_map, back) for pick_map, back in zip(maps[:-1], backs[:-1])]
    return finish(maps[-1], backs[-1], gate_scale, picked)


def solution(mesh):
    in_specs = (
        P("expert", "tensor"),
        P("expert"),
        P("expert"),
        P("expert", None, "tensor"),
        P("expert", None, "tensor"),
        P("expert", "tensor", None),
    )
    out_specs = P("expert", "tensor")
    return jax.shard_map(shards, mesh=mesh, in_specs=in_specs, out_specs=out_specs, check_vma=False)
```

```python
import functools

import jax
import jax.numpy as jnp
from jax import lax
from jax.experimental import pallas as pl
from jax.experimental.pallas import tpu as pltpu
from jax.sharding import PartitionSpec as P

F32 = jnp.float32
BF16 = jnp.bfloat16
MIB = 1 << 20


def vmem():
    return pl.BlockSpec(memory_space=pltpu.VMEM)


def in_hbm(array):
    return pltpu.with_memory_space_constraint(array, pltpu.HBM)


def exchange_order(n_expert):
    if n_expert == 16:
        return [10, 4, 9, 8, 5, 6, 11, 0, 12, 7, 13, 14, 1, 2, 15, 3]
    if n_expert % 4:
        return list(range(n_expert))
    quarter = [list(range(q * n_expert // 4, (q + 1) * n_expert // 4)) for q in range(4)]
    return [e for first, second in ((1, 2), (0, 3)) for pair in zip(quarter[first], quarter[second]) for e in pair]


def exchange_place(expert, n_expert):
    place = jnp.zeros_like(expert)
    for index, owner in enumerate(exchange_order(n_expert)):
        place = jnp.where(expert == owner, index, place)
    return place


def params(limit_mib):
    return pltpu.CompilerParams(vmem_limit_bytes=limit_mib * MIB)


def chunk_sizes(capacity):
    if capacity >= 32:
        return (capacity // 2, capacity // 2)
    return (capacity,)


def dispatch_kernel(n_expert, chunks, ids_hbm, tok_hbm, *refs):
    out_refs = refs[:len(chunks)]
    ids_ref, tok_ref, *stage_refs, arrived = refs[len(chunks):]
    copies = [
        pltpu.make_async_copy(ids_hbm, ids_ref, arrived.at[0]),
        pltpu.make_async_copy(tok_hbm, tok_ref, arrived.at[1]),
    ]
    for copy in copies:
        copy.start()
    n_tok = tok_ref.shape[0]
    owner = lax.broadcasted_iota(jnp.int32, (n_expert, n_tok), 0)
    before = lax.broadcasted_iota(jnp.int32, (n_tok, n_tok), 0) < lax.broadcasted_iota(jnp.int32, (n_tok, n_tok), 1)
    before = before.astype(F32).astype(BF16)
    copies[0].wait()
    ids = exchange_place(ids_ref[...], n_expert)
    onehot = (owner == ids).astype(F32)
    earlier = jnp.dot(onehot.astype(BF16), before, preferred_element_type=F32)
    rank = jnp.sum(earlier * onehot, axis=0, keepdims=True).astype(jnp.int32)
    picks = []
    low = 0
    for size in chunks:
        inside = (rank >= low) & (rank < low + size)
        target = jnp.where(inside, ids * size + (rank - low), -1)
        slot = lax.broadcasted_iota(jnp.int32, (n_expert * size, n_tok), 0)
        picks.append((slot == target).astype(F32).astype(BF16))
        low += size
    copies[1].wait()
    leaving = []
    for index in reversed(range(len(chunks))):
        rows = jnp.dot(picks[index], tok_ref[...], preferred_element_type=F32).astype(BF16)
        if index == 0:
            out_refs[0][...] = rows
        else:
            stage_refs[index - 1][...] = rows
            leaving.append(pltpu.make_async_copy(stage_refs[index - 1], out_refs[index], arrived.at[1 + index]))
            leaving[-1].start()
    for copy in leaving:
        copy.wait()


def dispatch(ids, tokens, n_expert, chunks):
    n_tok, width = tokens.shape
    hbm = pl.BlockSpec(memory_space=pltpu.HBM)
    return pl.pallas_call(
        functools.partial(dispatch_kernel, n_expert, chunks),
        out_shape=[jax.ShapeDtypeStruct((n_expert * size, width), BF16) for size in chunks],
        in_specs=[hbm, hbm],
        out_specs=[vmem()] + [hbm for _ in chunks[1:]],
        scratch_shapes=[pltpu.VMEM((1, n_tok), jnp.int32), pltpu.VMEM((n_tok, width), BF16)]
        + [pltpu.VMEM((n_expert * size, width), BF16) for size in chunks[1:]]
        + [pltpu.SemaphoreType.DMA((1 + len(chunks),))],
        compiler_params=params(24),
        name="dispatch",
    )(in_hbm(ids.reshape(1, n_tok)), in_hbm(tokens))


def combine_map_kernel(n_expert, chunks, ids_ref, *out_refs):
    n_tok = ids_ref.shape[0]
    ids = exchange_place(ids_ref[...], n_expert)
    owner = lax.broadcasted_iota(jnp.int32, (n_tok, n_expert), 1)
    onehot = (owner == ids).astype(F32)
    before = lax.broadcasted_iota(jnp.int32, (n_tok, n_tok), 1) < lax.broadcasted_iota(jnp.int32, (n_tok, n_tok), 0)
    earlier = jnp.dot(before.astype(F32).astype(BF16), onehot.astype(BF16), preferred_element_type=F32)
    rank = jnp.sum(earlier * onehot, axis=1, keepdims=True).astype(jnp.int32)
    low = 0
    for size, out_ref in zip(chunks, out_refs):
        inside = (rank >= low) & (rank < low + size)
        target = jnp.where(inside, ids * size + (rank - low), -1)
        slot = lax.broadcasted_iota(jnp.int32, (n_tok, n_expert * size), 1)
        out_ref[...] = (slot == target).astype(F32).astype(BF16)
        low += size


def combine_map(ids, n_expert, chunks):
    n_tok = ids.shape[0]
    return pl.pallas_call(
        functools.partial(combine_map_kernel, n_expert, chunks),
        out_shape=[jax.ShapeDtypeStruct((n_tok, n_expert * size), BF16) for size in chunks],
        in_specs=[vmem()],
        out_specs=[vmem() for _ in chunks],
        compiler_params=params(24),
        name="combine_map",
    )(ids.reshape(n_tok, 1))


def pick_kernel(map_ref, back_ref, out_ref):
    out_ref[...] = jnp.dot(map_ref[...], back_ref[...], preferred_element_type=F32).astype(BF16)


def pick(pick_map, back):
    return pl.pallas_call(
        pick_kernel,
        out_shape=jax.ShapeDtypeStruct((pick_map.shape[0], back.shape[1]), BF16),
        in_specs=[vmem(), vmem()],
        out_specs=vmem(),
        compiler_params=params(16),
        name="pick",
    )(pick_map, back)


def finish_kernel(n_part, map_ref, back_ref, scale_ref, *refs):
    part_refs = refs[:n_part]
    out_hbm, stage_ref, left = refs[n_part:]
    copies = []
    for index, cut in enumerate(row_cuts(stage_ref.shape[0])):
        total = jnp.dot(map_ref[cut, :], back_ref[...], preferred_element_type=F32)
        for part_ref in part_refs:
            total = total + part_ref[cut, :].astype(F32)
        stage_ref[cut, :] = (scale_ref[cut, :] * total).astype(BF16)
        copies.append(pltpu.make_async_copy(stage_ref.at[cut, :], out_hbm.at[cut, :], left.at[index]))
        copies[-1].start()
    for copy in copies:
        copy.wait()


def finish(pick_map, back, scale, parts):
    n_tok = pick_map.shape[0]
    shape = (n_tok, back.shape[1])
    return pl.pallas_call(
        functools.partial(finish_kernel, len(parts)),
        out_shape=jax.ShapeDtypeStruct(shape, BF16),
        in_specs=[vmem() for _ in range(3 + len(parts))],
        out_specs=pl.BlockSpec(memory_space=pltpu.HBM),
        scratch_shapes=[pltpu.VMEM(shape, BF16), pltpu.SemaphoreType.DMA((len(row_cuts(n_tok)),))],
        compiler_params=params(16),
        name="finish",
    )(pick_map, back, scale.reshape(n_tok, 1), *parts)


def expert_kernel(n_tensor, blocks, where_ref, *refs):
    part_refs = refs[:n_tensor]
    sources = refs[n_tensor:n_tensor + 3]
    out_refs = refs[n_tensor + 3:2 * n_tensor + 3]
    gate_ref, up_ref, down_ref, rows_ref, hidden_ref, arrived = refs[2 * n_tensor + 3:]
    width = part_refs[0].shape[1]
    me = where_ref[0]

    def columns(shift):
        return pl.ds(pl.multiple_of(lax.rem(me + shift, n_tensor) * width, width), width)

    fetches = []
    low = 0
    for step, size in enumerate(blocks):
        cut = pl.ds(low, size)
        fetches.append(
            (
                cut,
                pltpu.make_async_copy(sources[0].at[0, :, cut], gate_ref.at[:, cut], arrived.at[2 * step]),
                pltpu.make_async_copy(sources[1].at[0, :, cut], up_ref.at[:, cut], arrived.at[2 * step + 1]),
            )
        )
        low += size
    down_here = pltpu.make_async_copy(sources[2].at[0], down_ref, arrived.at[2 * len(blocks)])
    for _, gate_here, up_here in fetches:
        gate_here.start()
        up_here.start()
    down_here.start()
    for shift, part_ref in enumerate(part_refs):
        rows_ref[:, columns(shift)] = part_ref[...]
    for cut, gate_here, up_here in fetches:
        rows = rows_ref[...]
        gate_here.wait()
        gate = jnp.dot(rows, gate_ref[:, cut], preferred_element_type=F32)
        up_here.wait()
        up = jnp.dot(rows, up_ref[:, cut], preferred_element_type=F32)
        hidden_ref[:, cut] = (gate / (1.0 + jnp.exp(-gate)) * up).astype(BF16)
    down_here.wait()
    for shift, out_ref in enumerate(out_refs):
        share = jnp.dot(hidden_ref[...], down_ref[:, columns(shift)], preferred_element_type=F32)
        out_ref[...] = share.astype(BF16)


def expert_rows(where, parts, weights):
    n_tensor = len(parts)
    rows, width = parts[0].shape
    depth, hidden = weights[0].shape[1:]
    first = hidden // 3 // 128 * 128
    blocks = (first, hidden - first)
    hbm = pl.BlockSpec(memory_space=pltpu.HBM)
    return pl.pallas_call(
        functools.partial(expert_kernel, n_tensor, blocks),
        out_shape=[jax.ShapeDtypeStruct((rows, width), BF16) for _ in parts],
        in_specs=[pl.BlockSpec(memory_space=pltpu.SMEM)] + [vmem() for _ in parts] + [hbm, hbm, hbm],
        out_specs=[vmem() for _ in parts],
        scratch_shapes=[
            pltpu.VMEM((depth, hidden), BF16),
            pltpu.VMEM((depth, hidden), BF16),
            pltpu.VMEM((hidden, depth), BF16),
            pltpu.VMEM((rows, depth), BF16),
            pltpu.VMEM((rows, hidden), BF16),
            pltpu.SemaphoreType.DMA((2 * len(blocks) + 1,)),
        ],
        compiler_params=params(44),
        cost_estimate=pl.CostEstimate(
            flops=6 * rows * depth * hidden, bytes_accessed=6 * depth * hidden, transcendentals=rows * hidden
        ),
        name="expert_rows",
    )(where, *parts, *[in_hbm(weight) for weight in weights])


def row_cuts(rows):
    cut = rows // 4 if rows % 64 == 0 else rows
    return [pl.ds(low, cut) for low in range(0, rows, cut)]


def add_kernel(*refs):
    *share_refs, out_hbm, stage_ref, left = refs
    copies = []
    for index, cut in enumerate(row_cuts(stage_ref.shape[0])):
        total = share_refs[0][cut, :].astype(F32)
        for share_ref in share_refs[1:]:
            total = total + share_ref[cut, :].astype(F32)
        stage_ref[cut, :] = total.astype(BF16)
        copies.append(pltpu.make_async_copy(stage_ref.at[cut, :], out_hbm.at[cut, :], left.at[index]))
        copies[-1].start()
    for copy in copies:
        copy.wait()


def add(shares):
    shape = shares[0].shape
    return pl.pallas_call(
        add_kernel,
        out_shape=jax.ShapeDtypeStruct(shape, BF16),
        in_specs=[vmem() for _ in shares],
        out_specs=pl.BlockSpec(memory_space=pltpu.HBM),
        scratch_shapes=[pltpu.VMEM(shape, BF16), pltpu.SemaphoreType.DMA((len(row_cuts(shape[0])),))],
        compiler_params=params(8),
        name="add_shares",
    )(*shares)


def exchange(rows, n_expert):
    size = rows.shape[0] // n_expert
    moved = lax.all_to_all(
        rows.reshape(n_expert, size, -1),
        "expert",
        split_axis=0,
        concat_axis=0,
        axis_index_groups=[exchange_order(n_expert)],
        tiled=True,
    )
    return moved.reshape(rows.shape)


def shards(tokens, expert_ids, gate_scale, gate_weight, up_weight, down_weight):
    n_expert = lax.axis_size("expert")
    n_tensor = lax.axis_size("tensor")
    chunks = chunk_sizes(2 * tokens.shape[0] // n_expert)
    where = lax.axis_index("tensor").astype(jnp.int32).reshape(1)

    def shifted(rows, shift):
        return lax.ppermute(rows, "tensor", [(i, (i - shift) % n_tensor) for i in range(n_tensor)])

    outgoing = dispatch(expert_ids, tokens, n_expert, chunks)
    maps = combine_map(expert_ids, n_expert, chunks)
    weights = (gate_weight, up_weight, down_weight)
    backs = []
    for rows in outgoing:
        arrived = exchange(rows, n_expert)
        parts = [arrived] + [shifted(arrived, shift) for shift in range(1, n_tensor)]
        shares = expert_rows(where, parts, weights)
        total = add([shares[0]] + [shifted(shares[shift], -shift) for shift in range(1, n_tensor)])
        backs.append(exchange(total, n_expert))
    picked = [pick(pick_map, back) for pick_map, back in zip(maps[:-1], backs[:-1])]
    return finish(maps[-1], backs[-1], gate_scale, picked)


def solution(mesh):
    in_specs = (
        P("expert", "tensor"),
        P("expert"),
        P("expert"),
        P("expert", None, "tensor"),
        P("expert", None, "tensor"),
        P("expert", "tensor", None),
    )
    out_specs = P("expert", "tensor")
    return jax.shard_map(shards, mesh=mesh, in_specs=in_specs, out_specs=out_specs, check_vma=False)
```

```python
import functools

import jax
import jax.numpy as jnp
from jax import lax
from jax.experimental import pallas as pl
from jax.experimental.pallas import tpu as pltpu
from jax.sharding import PartitionSpec as P

F32 = jnp.float32
BF16 = jnp.bfloat16
MIB = 1 << 20


def vmem():
    return pl.BlockSpec(memory_space=pltpu.VMEM)


def in_hbm(array):
    return pltpu.with_memory_space_constraint(array, pltpu.HBM)


def exchange_order(n_expert):
    if n_expert == 16:
        return [10, 4, 9, 8, 5, 6, 11, 0, 12, 7, 13, 14, 1, 2, 15, 3]
    if n_expert % 4:
        return list(range(n_expert))
    quarter = [list(range(q * n_expert // 4, (q + 1) * n_expert // 4)) for q in range(4)]
    return [e for first, second in ((1, 2), (0, 3)) for pair in zip(quarter[first], quarter[second]) for e in pair]


def exchange_place(expert, n_expert):
    place = jnp.zeros_like(expert)
    for index, owner in enumerate(exchange_order(n_expert)):
        place = jnp.where(expert == owner, index, place)
    return place


def params(limit_mib):
    return pltpu.CompilerParams(vmem_limit_bytes=limit_mib * MIB)


def chunk_sizes(capacity):
    if capacity >= 32:
        return (capacity // 2, capacity // 2)
    return (capacity,)


def dispatch_kernel(n_expert, chunks, ids_hbm, tok_hbm, *refs):
    out_refs = refs[:len(chunks)]
    ids_ref, tok_ref, *stage_refs, arrived = refs[len(chunks):]
    copies = [
        pltpu.make_async_copy(ids_hbm, ids_ref, arrived.at[0]),
        pltpu.make_async_copy(tok_hbm, tok_ref, arrived.at[1]),
    ]
    for copy in copies:
        copy.start()
    n_tok = tok_ref.shape[0]
    owner = lax.broadcasted_iota(jnp.int32, (n_expert, n_tok), 0)
    before = lax.broadcasted_iota(jnp.int32, (n_tok, n_tok), 0) < lax.broadcasted_iota(jnp.int32, (n_tok, n_tok), 1)
    before = before.astype(F32).astype(BF16)
    copies[0].wait()
    ids = exchange_place(ids_ref[...], n_expert)
    onehot = (owner == ids).astype(F32)
    earlier = jnp.dot(onehot.astype(BF16), before, preferred_element_type=F32)
    rank = jnp.sum(earlier * onehot, axis=0, keepdims=True).astype(jnp.int32)
    picks = []
    low = 0
    for size in chunks:
        inside = (rank >= low) & (rank < low + size)
        target = jnp.where(inside, ids * size + (rank - low), -1)
        slot = lax.broadcasted_iota(jnp.int32, (n_expert * size, n_tok), 0)
        picks.append((slot == target).astype(F32).astype(BF16))
        low += size
    copies[1].wait()
    leaving = []
    for index in reversed(range(len(chunks))):
        rows = jnp.dot(picks[index], tok_ref[...], preferred_element_type=F32).astype(BF16)
        if index == 0:
            out_refs[0][...] = rows
        else:
            stage_refs[index - 1][...] = rows
            leaving.append(pltpu.make_async_copy(stage_refs[index - 1], out_refs[index], arrived.at[1 + index]))
            leaving[-1].start()
    for copy in leaving:
        copy.wait()


def dispatch(ids, tokens, n_expert, chunks):
    n_tok, width = tokens.shape
    hbm = pl.BlockSpec(memory_space=pltpu.HBM)
    return pl.pallas_call(
        functools.partial(dispatch_kernel, n_expert, chunks),
        out_shape=[jax.ShapeDtypeStruct((n_expert * size, width), BF16) for size in chunks],
        in_specs=[hbm, hbm],
        out_specs=[vmem()] + [hbm for _ in chunks[1:]],
        scratch_shapes=[pltpu.VMEM((1, n_tok), jnp.int32), pltpu.VMEM((n_tok, width), BF16)]
        + [pltpu.VMEM((n_expert * size, width), BF16) for size in chunks[1:]]
        + [pltpu.SemaphoreType.DMA((1 + len(chunks),))],
        compiler_params=params(24),
        name="dispatch",
    )(in_hbm(ids.reshape(1, n_tok)), in_hbm(tokens))


def combine_map_kernel(n_expert, chunks, ids_ref, *out_refs):
    n_tok = ids_ref.shape[0]
    ids = exchange_place(ids_ref[...], n_expert)
    owner = lax.broadcasted_iota(jnp.int32, (n_tok, n_expert), 1)
    onehot = (owner == ids).astype(F32)
    before = lax.broadcasted_iota(jnp.int32, (n_tok, n_tok), 1) < lax.broadcasted_iota(jnp.int32, (n_tok, n_tok), 0)
    earlier = jnp.dot(before.astype(F32).astype(BF16), onehot.astype(BF16), preferred_element_type=F32)
    rank = jnp.sum(earlier * onehot, axis=1, keepdims=True).astype(jnp.int32)
    low = 0
    for size, out_ref in zip(chunks, out_refs):
        inside = (rank >= low) & (rank < low + size)
        target = jnp.where(inside, ids * size + (rank - low), -1)
        slot = lax.broadcasted_iota(jnp.int32, (n_tok, n_expert * size), 1)
        out_ref[...] = (slot == target).astype(F32).astype(BF16)
        low += size


def combine_map(ids, n_expert, chunks):
    n_tok = ids.shape[0]
    return pl.pallas_call(
        functools.partial(combine_map_kernel, n_expert, chunks),
        out_shape=[jax.ShapeDtypeStruct((n_tok, n_expert * size), BF16) for size in chunks],
        in_specs=[vmem()],
        out_specs=[vmem() for _ in chunks],
        compiler_params=params(24),
        name="combine_map",
    )(ids.reshape(n_tok, 1))


def pick_kernel(map_ref, back_ref, out_ref):
    out_ref[...] = jnp.dot(map_ref[...], back_ref[...], preferred_element_type=F32).astype(BF16)


def pick(pick_map, back):
    return pl.pallas_call(
        pick_kernel,
        out_shape=jax.ShapeDtypeStruct((pick_map.shape[0], back.shape[1]), BF16),
        in_specs=[vmem(), vmem()],
        out_specs=vmem(),
        compiler_params=params(16),
        name="pick",
    )(pick_map, back)


def finish_kernel(n_part, map_ref, back_ref, scale_ref, *refs):
    part_refs = refs[:n_part]
    out_hbm, stage_ref, left = refs[n_part:]
    copies = []
    for index, cut in enumerate(row_cuts(stage_ref.shape[0])):
        total = jnp.dot(map_ref[cut, :], back_ref[...], preferred_element_type=F32)
        for part_ref in part_refs:
            total = total + part_ref[cut, :].astype(F32)
        stage_ref[cut, :] = (scale_ref[cut, :] * total).astype(BF16)
        copies.append(pltpu.make_async_copy(stage_ref.at[cut, :], out_hbm.at[cut, :], left.at[index]))
        copies[-1].start()
    for copy in copies:
        copy.wait()


def finish(pick_map, back, scale, parts):
    n_tok = pick_map.shape[0]
    shape = (n_tok, back.shape[1])
    return pl.pallas_call(
        functools.partial(finish_kernel, len(parts)),
        out_shape=jax.ShapeDtypeStruct(shape, BF16),
        in_specs=[vmem() for _ in range(3 + len(parts))],
        out_specs=pl.BlockSpec(memory_space=pltpu.HBM),
        scratch_shapes=[pltpu.VMEM(shape, BF16), pltpu.SemaphoreType.DMA((len(row_cuts(n_tok)),))],
        compiler_params=params(16),
        name="finish",
    )(pick_map, back, scale.reshape(n_tok, 1), *parts)


def expert_kernel(n_tensor, blocks, where_ref, *refs):
    part_refs = refs[:n_tensor]
    sources = refs[n_tensor:n_tensor + 3]
    out_refs = refs[n_tensor + 3:2 * n_tensor + 3]
    gate_ref, up_ref, down_ref, rows_ref, hidden_ref, arrived = refs[2 * n_tensor + 3:]
    width = part_refs[0].shape[1]
    me = where_ref[0]

    def columns(shift):
        return pl.ds(pl.multiple_of(lax.rem(me + shift, n_tensor) * width, width), width)

    fetches = []
    low = 0
    for step, size in enumerate(blocks):
        cut = pl.ds(low, size)
        fetches.append(
            (
                cut,
                pltpu.make_async_copy(sources[0].at[0, :, cut], gate_ref.at[:, cut], arrived.at[2 * step]),
                pltpu.make_async_copy(sources[1].at[0, :, cut], up_ref.at[:, cut], arrived.at[2 * step + 1]),
            )
        )
        low += size
    down_here = pltpu.make_async_copy(sources[2].at[0], down_ref, arrived.at[2 * len(blocks)])
    for _, gate_here, up_here in fetches:
        gate_here.start()
        up_here.start()
    down_here.start()
    for shift, part_ref in enumerate(part_refs):
        rows_ref[:, columns(shift)] = part_ref[...]
    for cut, gate_here, up_here in fetches:
        rows = rows_ref[...]
        gate_here.wait()
        gate = jnp.dot(rows, gate_ref[:, cut], preferred_element_type=F32)
        up_here.wait()
        up = jnp.dot(rows, up_ref[:, cut], preferred_element_type=F32)
        hidden_ref[:, cut] = (gate / (1.0 + jnp.exp(-gate)) * up).astype(BF16)
    down_here.wait()
    for shift, out_ref in enumerate(out_refs):
        share = jnp.dot(hidden_ref[...], down_ref[:, columns(shift)], preferred_element_type=F32)
        out_ref[...] = share.astype(BF16)


def expert_rows(where, parts, weights):
    n_tensor = len(parts)
    rows, width = parts[0].shape
    depth, hidden = weights[0].shape[1:]
    first = hidden // 3 // 128 * 128
    blocks = (first, hidden - first)
    hbm = pl.BlockSpec(memory_space=pltpu.HBM)
    return pl.pallas_call(
        functools.partial(expert_kernel, n_tensor, blocks),
        out_shape=[jax.ShapeDtypeStruct((rows, width), BF16) for _ in parts],
        in_specs=[pl.BlockSpec(memory_space=pltpu.SMEM)] + [vmem() for _ in parts] + [hbm, hbm, hbm],
        out_specs=[vmem() for _ in parts],
        scratch_shapes=[
            pltpu.VMEM((depth, hidden), BF16),
            pltpu.VMEM((depth, hidden), BF16),
            pltpu.VMEM((hidden, depth), BF16),
            pltpu.VMEM((rows, depth), BF16),
            pltpu.VMEM((rows, hidden), BF16),
            pltpu.SemaphoreType.DMA((2 * len(blocks) + 1,)),
        ],
        compiler_params=params(44),
        cost_estimate=pl.CostEstimate(
            flops=6 * rows * depth * hidden, bytes_accessed=6 * depth * hidden, transcendentals=rows * hidden
        ),
        name="expert_rows",
    )(where, *parts, *[in_hbm(weight) for weight in weights])


def others_kernel(n_tensor, blocks, where_ref, *refs):
    part_refs = refs[:n_tensor]
    sources = refs[n_tensor:n_tensor + 3]
    hidden_ref, own_ref, *out_refs = refs[n_tensor + 3:2 * n_tensor + 4]
    gate_ref, up_ref, down_ref, rows_ref, arrived = refs[2 * n_tensor + 4:]
    width = part_refs[0].shape[1]
    me = where_ref[0]

    def columns(shift):
        return pl.ds(pl.multiple_of(lax.rem(me + shift, n_tensor) * width, width), width)

    fetches = []
    low = 0
    for step, size in enumerate(blocks):
        cut = pl.ds(low, size)
        fetches.append(
            (
                cut,
                pltpu.make_async_copy(sources[0].at[0, :, cut], gate_ref.at[:, cut], arrived.at[2 * step]),
                pltpu.make_async_copy(sources[1].at[0, :, cut], up_ref.at[:, cut], arrived.at[2 * step + 1]),
            )
        )
        low += size
    down_here = [
        pltpu.make_async_copy(
            sources[2].at[0, :, columns(shift)],
            own_ref if shift == 0 else down_ref.at[shift - 1],
            arrived.at[2 * len(blocks) + shift],
        )
        for shift in range(n_tensor)
    ]
    for _, gate_here, up_here in fetches:
        gate_here.start()
        up_here.start()
    for fetch in down_here[1:] + down_here[:1]:
        fetch.start()
    for shift, part_ref in enumerate(part_refs):
        rows_ref[:, columns(shift)] = part_ref[...]
    for cut, gate_here, up_here in fetches:
        rows = rows_ref[...]
        gate_here.wait()
        gate = jnp.dot(rows, gate_ref[:, cut], preferred_element_type=F32)
        up_here.wait()
        up = jnp.dot(rows, up_ref[:, cut], preferred_element_type=F32)
        hidden_ref[:, cut] = (gate / (1.0 + jnp.exp(-gate)) * up).astype(BF16)
    for shift, out_ref in enumerate(out_refs, 1):
        down_here[shift].wait()
        share = jnp.dot(hidden_ref[...], down_ref[shift - 1], preferred_element_type=F32)
        out_ref[...] = share.astype(BF16)
    down_here[0].wait()


def other_shares(where, parts, weights):
    n_tensor = len(parts)
    rows, width = parts[0].shape
    depth, hidden = weights[0].shape[1:]
    first = hidden // 3 // 128 * 128
    blocks = (first, hidden - first)
    hbm = pl.BlockSpec(memory_space=pltpu.HBM)
    hidden_rows, own_down, *others = pl.pallas_call(
        functools.partial(others_kernel, n_tensor, blocks),
        out_shape=[jax.ShapeDtypeStruct((rows, hidden), BF16), jax.ShapeDtypeStruct((hidden, width), BF16)]
        + [jax.ShapeDtypeStruct((rows, width), BF16) for _ in parts[1:]],
        in_specs=[pl.BlockSpec(memory_space=pltpu.SMEM)] + [vmem() for _ in parts] + [hbm, hbm, hbm],
        out_specs=[vmem() for _ in range(1 + n_tensor)],
        scratch_shapes=[
            pltpu.VMEM((depth, hidden), BF16),
            pltpu.VMEM((depth, hidden), BF16),
            pltpu.VMEM((max(n_tensor - 1, 1), hidden, width), BF16),
            pltpu.VMEM((rows, depth), BF16),
            pltpu.SemaphoreType.DMA((2 * len(blocks) + n_tensor,)),
        ],
        compiler_params=params(36),
        cost_estimate=pl.CostEstimate(
            flops=4 * rows * depth * hidden + 2 * rows * (depth - width) * hidden,
            bytes_accessed=6 * depth * hidden,
            transcendentals=rows * hidden,
        ),
        name="other_shares",
    )(where, *parts, *[in_hbm(weight) for weight in weights])
    return hidden_rows, own_down, others


def own_share_kernel(hidden_ref, down_ref, out_ref):
    out_ref[...] = jnp.dot(hidden_ref[...], down_ref[...], preferred_element_type=F32).astype(BF16)


def own_share(hidden_rows, own_down):
    rows, hidden = hidden_rows.shape
    width = own_down.shape[1]
    return pl.pallas_call(
        own_share_kernel,
        out_shape=jax.ShapeDtypeStruct((rows, width), BF16),
        in_specs=[vmem(), vmem()],
        out_specs=vmem(),
        compiler_params=params(16),
        cost_estimate=pl.CostEstimate(
            flops=2 * rows * width * hidden, bytes_accessed=2 * hidden * (rows + width), transcendentals=0
        ),
        name="own_share",
    )(hidden_rows, own_down)


def row_cuts(rows):
    cut = rows // 4 if rows % 64 == 0 else rows
    return [pl.ds(low, cut) for low in range(0, rows, cut)]


def add_kernel(*refs):
    *share_refs, out_hbm, stage_ref, left = refs
    copies = []
    for index, cut in enumerate(row_cuts(stage_ref.shape[0])):
        total = share_refs[0][cut, :].astype(F32)
        for share_ref in share_refs[1:]:
            total = total + share_ref[cut, :].astype(F32)
        stage_ref[cut, :] = total.astype(BF16)
        copies.append(pltpu.make_async_copy(stage_ref.at[cut, :], out_hbm.at[cut, :], left.at[index]))
        copies[-1].start()
    for copy in copies:
        copy.wait()


def add(shares):
    shape = shares[0].shape
    return pl.pallas_call(
        add_kernel,
        out_shape=jax.ShapeDtypeStruct(shape, BF16),
        in_specs=[vmem() for _ in shares],
        out_specs=pl.BlockSpec(memory_space=pltpu.HBM),
        scratch_shapes=[pltpu.VMEM(shape, BF16), pltpu.SemaphoreType.DMA((len(row_cuts(shape[0])),))],
        compiler_params=params(8),
        name="add_shares",
    )(*shares)


def exchange(rows, n_expert):
    size = rows.shape[0] // n_expert
    moved = lax.all_to_all(
        rows.reshape(n_expert, size, -1),
        "expert",
        split_axis=0,
        concat_axis=0,
        axis_index_groups=[exchange_order(n_expert)],
        tiled=True,
    )
    return moved.reshape(rows.shape)


def shards(tokens, expert_ids, gate_scale, gate_weight, up_weight, down_weight):
    n_expert = lax.axis_size("expert")
    n_tensor = lax.axis_size("tensor")
    chunks = chunk_sizes(2 * tokens.shape[0] // n_expert)
    where = lax.axis_index("tensor").astype(jnp.int32).reshape(1)

    def shifted(rows, shift):
        return lax.ppermute(rows, "tensor", [(i, (i - shift) % n_tensor) for i in range(n_tensor)])

    outgoing = dispatch(expert_ids, tokens, n_expert, chunks)
    maps = combine_map(expert_ids, n_expert, chunks)
    weights = (gate_weight, up_weight, down_weight)
    backs = []
    for index, rows in enumerate(outgoing):
        arrived = exchange(rows, n_expert)
        parts = [arrived] + [shifted(arrived, shift) for shift in range(1, n_tensor)]
        if index < len(outgoing) - 1:
            own, *others = expert_rows(where, parts, weights)
            received = [shifted(share, -shift) for shift, share in enumerate(others, 1)]
        else:
            hidden_rows, own_down, others = other_shares(where, parts, weights)
            received = [shifted(share, -shift) for shift, share in enumerate(others, 1)]
            own = own_share(hidden_rows, own_down)
        total = add([own] + received)
        backs.append(exchange(total, n_expert))
    picked = [pick(pick_map, back) for pick_map, back in zip(maps[:-1], backs[:-1])]
    return finish(maps[-1], backs[-1], gate_scale, picked)


def solution(mesh):
    in_specs = (
        P("expert", "tensor"),
        P("expert"),
        P("expert"),
        P("expert", None, "tensor"),
        P("expert", None, "tensor"),
        P("expert", "tensor", None),
    )
    out_specs = P("expert", "tensor")
    return jax.shard_map(shards, mesh=mesh, in_specs=in_specs, out_specs=out_specs, check_vma=False)
```

```python
import functools

import jax
import jax.numpy as jnp
from jax import lax
from jax.experimental import pallas as pl
from jax.experimental.pallas import tpu as pltpu
from jax.sharding import PartitionSpec as P

F32 = jnp.float32
BF16 = jnp.bfloat16
MIB = 1 << 20


def vmem():
    return pl.BlockSpec(memory_space=pltpu.VMEM)


def in_hbm(array):
    return pltpu.with_memory_space_constraint(array, pltpu.HBM)


def exchange_order(n_expert):
    if n_expert == 16:
        return [10, 4, 9, 8, 5, 6, 11, 0, 12, 7, 13, 14, 1, 2, 15, 3]
    if n_expert % 4:
        return list(range(n_expert))
    quarter = [list(range(q * n_expert // 4, (q + 1) * n_expert // 4)) for q in range(4)]
    return [e for first, second in ((1, 2), (0, 3)) for pair in zip(quarter[first], quarter[second]) for e in pair]


def exchange_place(expert, n_expert):
    place = jnp.zeros_like(expert)
    for index, owner in enumerate(exchange_order(n_expert)):
        place = jnp.where(expert == owner, index, place)
    return place


def params(limit_mib):
    return pltpu.CompilerParams(vmem_limit_bytes=limit_mib * MIB)


def chunk_sizes(capacity):
    if capacity >= 32:
        return (capacity // 2, capacity // 2)
    return (capacity,)


def dispatch_kernel(n_expert, chunks, ids_hbm, tok_hbm, *refs):
    out_refs = refs[:len(chunks)]
    ids_ref, tok_ref, *stage_refs, arrived = refs[len(chunks):]
    copies = [
        pltpu.make_async_copy(ids_hbm, ids_ref, arrived.at[0]),
        pltpu.make_async_copy(tok_hbm, tok_ref, arrived.at[1]),
    ]
    for copy in copies:
        copy.start()
    n_tok = tok_ref.shape[0]
    owner = lax.broadcasted_iota(jnp.int32, (n_expert, n_tok), 0)
    before = lax.broadcasted_iota(jnp.int32, (n_tok, n_tok), 0) < lax.broadcasted_iota(jnp.int32, (n_tok, n_tok), 1)
    before = before.astype(F32).astype(BF16)
    copies[0].wait()
    ids = exchange_place(ids_ref[...], n_expert)
    onehot = (owner == ids).astype(F32)
    earlier = jnp.dot(onehot.astype(BF16), before, preferred_element_type=F32)
    rank = jnp.sum(earlier * onehot, axis=0, keepdims=True).astype(jnp.int32)
    picks = []
    low = 0
    for size in chunks:
        inside = (rank >= low) & (rank < low + size)
        target = jnp.where(inside, ids * size + (rank - low), -1)
        slot = lax.broadcasted_iota(jnp.int32, (n_expert * size, n_tok), 0)
        picks.append((slot == target).astype(F32).astype(BF16))
        low += size
    copies[1].wait()
    leaving = []
    for index in reversed(range(len(chunks))):
        rows = jnp.dot(picks[index], tok_ref[...], preferred_element_type=F32).astype(BF16)
        if index == 0:
            out_refs[0][...] = rows
        else:
            stage_refs[index - 1][...] = rows
            leaving.append(pltpu.make_async_copy(stage_refs[index - 1], out_refs[index], arrived.at[1 + index]))
            leaving[-1].start()
    for copy in leaving:
        copy.wait()


def dispatch(ids, tokens, n_expert, chunks):
    n_tok, width = tokens.shape
    hbm = pl.BlockSpec(memory_space=pltpu.HBM)
    return pl.pallas_call(
        functools.partial(dispatch_kernel, n_expert, chunks),
        out_shape=[jax.ShapeDtypeStruct((n_expert * size, width), BF16) for size in chunks],
        in_specs=[hbm, hbm],
        out_specs=[vmem()] + [hbm for _ in chunks[1:]],
        scratch_shapes=[pltpu.VMEM((1, n_tok), jnp.int32), pltpu.VMEM((n_tok, width), BF16)]
        + [pltpu.VMEM((n_expert * size, width), BF16) for size in chunks[1:]]
        + [pltpu.SemaphoreType.DMA((1 + len(chunks),))],
        compiler_params=params(24),
        name="dispatch",
    )(in_hbm(ids.reshape(1, n_tok)), in_hbm(tokens))


def combine_map_kernel(n_expert, chunks, ids_ref, *out_refs):
    n_tok = ids_ref.shape[0]
    ids = exchange_place(ids_ref[...], n_expert)
    owner = lax.broadcasted_iota(jnp.int32, (n_tok, n_expert), 1)
    onehot = (owner == ids).astype(F32)
    before = lax.broadcasted_iota(jnp.int32, (n_tok, n_tok), 1) < lax.broadcasted_iota(jnp.int32, (n_tok, n_tok), 0)
    earlier = jnp.dot(before.astype(F32).astype(BF16), onehot.astype(BF16), preferred_element_type=F32)
    rank = jnp.sum(earlier * onehot, axis=1, keepdims=True).astype(jnp.int32)
    low = 0
    for size, out_ref in zip(chunks, out_refs):
        inside = (rank >= low) & (rank < low + size)
        target = jnp.where(inside, ids * size + (rank - low), -1)
        slot = lax.broadcasted_iota(jnp.int32, (n_tok, n_expert * size), 1)
        out_ref[...] = (slot == target).astype(F32).astype(BF16)
        low += size


def combine_map(ids, n_expert, chunks):
    n_tok = ids.shape[0]
    return pl.pallas_call(
        functools.partial(combine_map_kernel, n_expert, chunks),
        out_shape=[jax.ShapeDtypeStruct((n_tok, n_expert * size), BF16) for size in chunks],
        in_specs=[vmem()],
        out_specs=[vmem() for _ in chunks],
        compiler_params=params(24),
        name="combine_map",
    )(ids.reshape(n_tok, 1))


def pick_kernel(map_ref, back_ref, out_ref):
    out_ref[...] = jnp.dot(map_ref[...], back_ref[...], preferred_element_type=F32).astype(BF16)


def pick(pick_map, back):
    return pl.pallas_call(
        pick_kernel,
        out_shape=jax.ShapeDtypeStruct((pick_map.shape[0], back.shape[1]), BF16),
        in_specs=[vmem(), vmem()],
        out_specs=vmem(),
        compiler_params=params(16),
        name="pick",
    )(pick_map, back)


def finish_kernel(n_part, map_ref, back_ref, scale_ref, *refs):
    part_refs = refs[:n_part]
    out_hbm, stage_ref, left = refs[n_part:]
    copies = []
    for index, cut in enumerate(row_cuts(stage_ref.shape[0])):
        total = jnp.dot(map_ref[cut, :], back_ref[...], preferred_element_type=F32)
        for part_ref in part_refs:
            total = total + part_ref[cut, :].astype(F32)
        stage_ref[cut, :] = (scale_ref[cut, :] * total).astype(BF16)
        copies.append(pltpu.make_async_copy(stage_ref.at[cut, :], out_hbm.at[cut, :], left.at[index]))
        copies[-1].start()
    for copy in copies:
        copy.wait()


def finish(pick_map, back, scale, parts):
    n_tok = pick_map.shape[0]
    shape = (n_tok, back.shape[1])
    return pl.pallas_call(
        functools.partial(finish_kernel, len(parts)),
        out_shape=jax.ShapeDtypeStruct(shape, BF16),
        in_specs=[vmem() for _ in range(3 + len(parts))],
        out_specs=pl.BlockSpec(memory_space=pltpu.HBM),
        scratch_shapes=[pltpu.VMEM(shape, BF16), pltpu.SemaphoreType.DMA((len(row_cuts(n_tok)),))],
        compiler_params=params(16),
        name="finish",
    )(pick_map, back, scale.reshape(n_tok, 1), *parts)


def expert_kernel(n_tensor, blocks, where_ref, *refs):
    part_refs = refs[:n_tensor]
    sources = refs[n_tensor:n_tensor + 3]
    out_refs = refs[n_tensor + 3:2 * n_tensor + 3]
    gate_ref, up_ref, down_ref, rows_ref, hidden_ref, arrived = refs[2 * n_tensor + 3:]
    width = part_refs[0].shape[1]
    me = where_ref[0]

    def columns(shift):
        return pl.ds(pl.multiple_of(lax.rem(me + shift, n_tensor) * width, width), width)

    fetches = []
    low = 0
    for step, size in enumerate(blocks):
        cut = pl.ds(low, size)
        fetches.append(
            (
                cut,
                pltpu.make_async_copy(sources[0].at[0, :, cut], gate_ref.at[:, cut], arrived.at[2 * step]),
                pltpu.make_async_copy(sources[1].at[0, :, cut], up_ref.at[:, cut], arrived.at[2 * step + 1]),
            )
        )
        low += size
    down_here = pltpu.make_async_copy(sources[2].at[0], down_ref, arrived.at[2 * len(blocks)])
    for _, gate_here, up_here in fetches:
        gate_here.start()
        up_here.start()
    down_here.start()
    for shift, part_ref in enumerate(part_refs):
        rows_ref[:, columns(shift)] = part_ref[...]
    for cut, gate_here, up_here in fetches:
        rows = rows_ref[...]
        gate_here.wait()
        gate = jnp.dot(rows, gate_ref[:, cut], preferred_element_type=F32)
        up_here.wait()
        up = jnp.dot(rows, up_ref[:, cut], preferred_element_type=F32)
        hidden_ref[:, cut] = (gate / (1.0 + jnp.exp(-gate)) * up).astype(BF16)
    down_here.wait()
    for shift, out_ref in enumerate(out_refs):
        share = jnp.dot(hidden_ref[...], down_ref[:, columns(shift)], preferred_element_type=F32)
        out_ref[...] = share.astype(BF16)


def expert_rows(where, parts, weights):
    n_tensor = len(parts)
    rows, width = parts[0].shape
    depth, hidden = weights[0].shape[1:]
    first = hidden // 3 // 128 * 128
    blocks = (first, hidden - first)
    hbm = pl.BlockSpec(memory_space=pltpu.HBM)
    return pl.pallas_call(
        functools.partial(expert_kernel, n_tensor, blocks),
        out_shape=[jax.ShapeDtypeStruct((rows, width), BF16) for _ in parts],
        in_specs=[pl.BlockSpec(memory_space=pltpu.SMEM)] + [vmem() for _ in parts] + [hbm, hbm, hbm],
        out_specs=[vmem() for _ in parts],
        scratch_shapes=[
            pltpu.VMEM((depth, hidden), BF16),
            pltpu.VMEM((depth, hidden), BF16),
            pltpu.VMEM((hidden, depth), BF16),
            pltpu.VMEM((rows, depth), BF16),
            pltpu.VMEM((rows, hidden), BF16),
            pltpu.SemaphoreType.DMA((2 * len(blocks) + 1,)),
        ],
        compiler_params=params(44),
        cost_estimate=pl.CostEstimate(
            flops=6 * rows * depth * hidden, bytes_accessed=6 * depth * hidden, transcendentals=rows * hidden
        ),
        name="expert_rows",
    )(where, *parts, *[in_hbm(weight) for weight in weights])


def others_kernel(n_tensor, blocks, where_ref, *refs):
    part_refs = refs[:n_tensor]
    sources = refs[n_tensor:n_tensor + 3]
    hidden_ref, own_ref, *out_refs = refs[n_tensor + 3:2 * n_tensor + 4]
    gate_ref, up_ref, down_ref, rows_ref, arrived = refs[2 * n_tensor + 4:]
    width = part_refs[0].shape[1]
    me = where_ref[0]

    def columns(shift):
        return pl.ds(pl.multiple_of(lax.rem(me + shift, n_tensor) * width, width), width)

    fetches = []
    low = 0
    for step, size in enumerate(blocks):
        cut = pl.ds(low, size)
        fetches.append(
            (
                cut,
                pltpu.make_async_copy(sources[0].at[0, :, cut], gate_ref.at[:, cut], arrived.at[2 * step]),
                pltpu.make_async_copy(sources[1].at[0, :, cut], up_ref.at[:, cut], arrived.at[2 * step + 1]),
            )
        )
        low += size
    down_here = [
        pltpu.make_async_copy(
            sources[2].at[0, :, columns(shift)],
            own_ref if shift == 0 else down_ref.at[shift - 1],
            arrived.at[2 * len(blocks) + shift],
        )
        for shift in range(n_tensor)
    ]
    for _, gate_here, up_here in fetches:
        gate_here.start()
        up_here.start()
    for fetch in down_here[1:] + down_here[:1]:
        fetch.start()
    for shift, part_ref in enumerate(part_refs):
        rows_ref[:, columns(shift)] = part_ref[...]
    for cut, gate_here, up_here in fetches:
        rows = rows_ref[...]
        gate_here.wait()
        gate = jnp.dot(rows, gate_ref[:, cut], preferred_element_type=F32)
        up_here.wait()
        up = jnp.dot(rows, up_ref[:, cut], preferred_element_type=F32)
        hidden_ref[:, cut] = (gate / (1.0 + jnp.exp(-gate)) * up).astype(BF16)
    for shift, out_ref in enumerate(out_refs, 1):
        down_here[shift].wait()
        share = jnp.dot(hidden_ref[...], down_ref[shift - 1], preferred_element_type=F32)
        out_ref[...] = share.astype(BF16)
    down_here[0].wait()


def other_shares(where, parts, weights):
    n_tensor = len(parts)
    rows, width = parts[0].shape
    depth, hidden = weights[0].shape[1:]
    first = hidden // 3 // 128 * 128
    blocks = (first, hidden - first)
    hbm = pl.BlockSpec(memory_space=pltpu.HBM)
    hidden_rows, own_down, *others = pl.pallas_call(
        functools.partial(others_kernel, n_tensor, blocks),
        out_shape=[jax.ShapeDtypeStruct((rows, hidden), BF16), jax.ShapeDtypeStruct((hidden, width), BF16)]
        + [jax.ShapeDtypeStruct((rows, width), BF16) for _ in parts[1:]],
        in_specs=[pl.BlockSpec(memory_space=pltpu.SMEM)] + [vmem() for _ in parts] + [hbm, hbm, hbm],
        out_specs=[vmem() for _ in range(1 + n_tensor)],
        scratch_shapes=[
            pltpu.VMEM((depth, hidden), BF16),
            pltpu.VMEM((depth, hidden), BF16),
            pltpu.VMEM((max(n_tensor - 1, 1), hidden, width), BF16),
            pltpu.VMEM((rows, depth), BF16),
            pltpu.SemaphoreType.DMA((2 * len(blocks) + n_tensor,)),
        ],
        compiler_params=params(36),
        cost_estimate=pl.CostEstimate(
            flops=4 * rows * depth * hidden + 2 * rows * (depth - width) * hidden,
            bytes_accessed=6 * depth * hidden,
            transcendentals=rows * hidden,
        ),
        name="other_shares",
    )(where, *parts, *[in_hbm(weight) for weight in weights])
    return hidden_rows, own_down, others


def own_share_kernel(hidden_ref, down_ref, out_ref):
    out_ref[...] = jnp.dot(hidden_ref[...], down_ref[...], preferred_element_type=F32).astype(BF16)


def own_share(hidden_rows, own_down):
    rows, hidden = hidden_rows.shape
    width = own_down.shape[1]
    return pl.pallas_call(
        own_share_kernel,
        out_shape=jax.ShapeDtypeStruct((rows, width), BF16),
        in_specs=[vmem(), vmem()],
        out_specs=vmem(),
        compiler_params=params(16),
        cost_estimate=pl.CostEstimate(
            flops=2 * rows * width * hidden, bytes_accessed=2 * hidden * (rows + width), transcendentals=0
        ),
        name="own_share",
    )(hidden_rows, own_down)


def row_cuts(rows):
    cut = rows // 2 if rows % 32 == 0 else rows
    return [pl.ds(low, cut) for low in range(0, rows, cut)]


def add_kernel(*refs):
    *share_refs, out_hbm, stage_ref, left = refs
    copies = []
    for index, cut in enumerate(row_cuts(stage_ref.shape[0])):
        total = share_refs[0][cut, :].astype(F32)
        for share_ref in share_refs[1:]:
            total = total + share_ref[cut, :].astype(F32)
        stage_ref[cut, :] = total.astype(BF16)
        copies.append(pltpu.make_async_copy(stage_ref.at[cut, :], out_hbm.at[cut, :], left.at[index]))
        copies[-1].start()
    for copy in copies:
        copy.wait()


def add(shares):
    shape = shares[0].shape
    return pl.pallas_call(
        add_kernel,
        out_shape=jax.ShapeDtypeStruct(shape, BF16),
        in_specs=[vmem() for _ in shares],
        out_specs=pl.BlockSpec(memory_space=pltpu.HBM),
        scratch_shapes=[pltpu.VMEM(shape, BF16), pltpu.SemaphoreType.DMA((len(row_cuts(shape[0])),))],
        compiler_params=params(8),
        name="add_shares",
    )(*shares)


def exchange(rows, n_expert):
    size = rows.shape[0] // n_expert
    moved = lax.all_to_all(
        rows.reshape(n_expert, size, -1),
        "expert",
        split_axis=0,
        concat_axis=0,
        axis_index_groups=[exchange_order(n_expert)],
        tiled=True,
    )
    return moved.reshape(rows.shape)


def shards(tokens, expert_ids, gate_scale, gate_weight, up_weight, down_weight):
    n_expert = lax.axis_size("expert")
    n_tensor = lax.axis_size("tensor")
    chunks = chunk_sizes(2 * tokens.shape[0] // n_expert)
    where = lax.axis_index("tensor").astype(jnp.int32).reshape(1)

    def shifted(rows, shift):
        return lax.ppermute(rows, "tensor", [(i, (i - shift) % n_tensor) for i in range(n_tensor)])

    outgoing = dispatch(expert_ids, tokens, n_expert, chunks)
    maps = combine_map(expert_ids, n_expert, chunks)
    weights = (gate_weight, up_weight, down_weight)
    backs = []
    for index, rows in enumerate(outgoing):
        arrived = exchange(rows, n_expert)
        parts = [arrived] + [shifted(arrived, shift) for shift in range(1, n_tensor)]
        if index < len(outgoing) - 1:
            own, *others = expert_rows(where, parts, weights)
            received = [shifted(share, -shift) for shift, share in enumerate(others, 1)]
        else:
            hidden_rows, own_down, others = other_shares(where, parts, weights)
            received = [shifted(share, -shift) for shift, share in enumerate(others, 1)]
            own = own_share(hidden_rows, own_down)
        total = add([own] + received)
        backs.append(exchange(total, n_expert))
    picked = [pick(pick_map, back) for pick_map, back in zip(maps[:-1], backs[:-1])]
    return finish(maps[-1], backs[-1], gate_scale, picked)


def solution(mesh):
    in_specs = (
        P("expert", "tensor"),
        P("expert"),
        P("expert"),
        P("expert", None, "tensor"),
        P("expert", None, "tensor"),
        P("expert", "tensor", None),
    )
    out_specs = P("expert", "tensor")
    return jax.shard_map(shards, mesh=mesh, in_specs=in_specs, out_specs=out_specs, check_vma=False)
```
